32 devices in a mesh: groups: 2 (over y), ctx: 4 (over z), exp: 4 (over x, core).
Axes of the slice: x: 2, y: 2, z: 4, core: 2. Of those that a mesh axis runs over, the one named last changes fastest.
Arguments:
- queries: bfloat16 [1024, 2048], P(('groups', 'ctx'), 'exp'), parts along dimension 0, may hold values from -10 to 10
- keys: bfloat16 [4096, 512], P(('groups', 'ctx'), 'exp'), parts along dimension 0, may hold values from -10 to 10
- values: bfloat16 [4096, 512], P(('groups', 'ctx'), 'exp'), parts along dimension 0, may hold values from -6 to 6
- out_weight: bfloat16 [2048, 4096], P('exp', 'ctx'), may hold values from -0.125 to 0.125
- residual: bfloat16 [1024, 4096], P(('groups', 'ctx'), 'exp'), parts along dimension 0, may hold values from -2 to 2
- router: float32 [4096, 4], replicated, may hold values from -0.09375 to 0.09375
- routes: int32 [1024, 2], P(('groups', 'ctx')), parts along dimension 0, may hold values from 0 to 3, all different within a row; in each aligned block of 128 rows (0 to 127, 128 to 255, ...) at most 64 rows name the same one
- order: int32 [1024], P(('groups', 'ctx')), parts along dimension 0, may hold values from 0 to 511, each once
- expert_gate: bfloat16 [4, 4096, 7168], P('exp', None, 'ctx'), may hold values from -0.09375 to 0.09375
- expert_up: bfloat16 [4, 4096, 7168], P('exp', None, 'ctx'), may hold values from -0.09375 to 0.09375
- expert_down: bfloat16 [4, 7168, 4096], P('exp', 'ctx'), may hold values from -0.0625 to 0.0625
Outputs:
- layer_output: bfloat16 [1024, 4096], P(('groups', 'ctx', 'exp')), parts along dimension 0
The draws below stay inside these ranges and needn't reach their ends.
There are 2 independent parts, one for each index of `groups`. The reference program is written for one: setup_inputs(seed, part) draws one part's arguments, and reference() takes and returns one part's arrays. A program takes and returns all parts, laid end to end along the dimension named above; an argument that names none is the same for every part. Nothing has to cross between parts.
Inputs may be any that keep to these rules, and one draw needn't show every extreme that they name: `routes`: in the 128 rows of one index of ctx, no expert is named by more than 64 rows, a bound that some block reaches; a row names two different experts.
All inputs are finite; a program needn't handle non-finite values.
Results may differ from the reference program's by a relative error of at most 0.022.
Values may be sent and summed in bfloat16 or wider, within the bound.
No kernel may reach another device: no remote copies, remote signals or barrier semaphores. Data moves between devices by JAX's collectives and lax.ppermute only.
A program may use at most 128 MiB of HBM per device.

```python
import math
import jax
import jax.numpy as jnp
import numpy as np
from jax import lax

D = 4096
HD = 128
QPK = 4
FF = 7168
TOK_DEV = 128
KV_HEADS = 4
HEADS = 16
EXPERTS = 4
MOST = 64
NEW = 512
CTX_LEN = 2048
N_CTX = 4


def draw_queries(key, part):
    key = jax.random.fold_in(key, 21)
    base = jnp.clip(1.5 * jax.random.normal(key, (NEW, KV_HEADS, QPK, HD), jnp.float32), -8.0, 8.0)
    return base.reshape(NEW, HEADS * HD).astype(jnp.bfloat16)


def draw_keys(key, part):
    key = jax.random.fold_in(key, 22)
    base = jnp.clip(1.5 * jax.random.normal(key, (CTX_LEN, KV_HEADS, HD), jnp.float32), -8.0, 8.0)
    return base.reshape(CTX_LEN, KV_HEADS * HD).astype(jnp.bfloat16)


def block_scale(key, shape, pieces, low, largest):
    gain, own = 1.0, jax.random.fold_in(key, 6)
    for position, shards_of in pieces:
        draws = jnp.exp(jax.random.uniform(jax.random.fold_in(own, position), (shards_of,), jnp.float32, low / len(pieces), largest / len(pieces)))
        gain = gain * jnp.repeat(draws, shape[position] // shards_of).reshape([-1 if axis == position else 1 for axis in range(len(shape))])
    return gain


def assign_block(stream_key, own, number, rows, number_of, top, limit, skew):
    ranking = jax.random.permutation(stream_key, number_of)
    crowded, ordinary = shares(number_of, rows * top, limit, skew, True), shares(number_of, rows * top, limit, skew, False)
    places = jnp.arange(number_of)

    def named(lengths, rotation):
        used = int((lengths > 0).sum())
        fixed = max(1, used // 4)
        shifted = fixed + (places - fixed + rotation * (used - fixed)) % max(1, number_of - fixed)
        return jnp.zeros((number_of,), jnp.int32).at[ranking[jnp.where(places < fixed, places, shifted)]].set(jnp.asarray(lengths, jnp.int32))

    lengths = jnp.where(number % 4 == 0, named(crowded, number // 4), named(ordinary, number - number // 4 - 1))
    mixed = jax.random.permutation(jax.random.fold_in(own, 3), number_of)
    source_of, sink = mixed[0:number_of // 2 * 2:2], mixed[1:number_of // 2 * 2:2]
    slack = jnp.minimum(lengths[source_of] - 1, limit - lengths[sink]) // 2
    slack = jnp.where((source_of == ranking[0]) | (sink == ranking[0]) | (lengths[sink] == 0), 0, jnp.maximum(slack, 0))
    shifted = jax.random.randint(jax.random.fold_in(own, 4), (number_of // 2,), 0, 1 << 20) % (slack + 1)
    lengths = lengths.at[source_of].add(-shifted).at[sink].add(shifted)
    labels = jnp.searchsorted(jnp.cumsum(lengths), jnp.arange(rows * top), side="right").astype(jnp.int32)
    grid = labels.reshape(top, rows).T
    grid = grid[jax.random.permutation(jax.random.fold_in(own, 1), rows)]
    rotation = jax.random.randint(jax.random.fold_in(own, 2), (rows, 1), 0, top)
    return jnp.take_along_axis(grid, (jnp.arange(top)[None, :] + rotation) % top, axis=1)


def shares(count, total, most, skew, full):
    loads = [(1 << 20) // math.isqrt(rank ** skew) + 1 for rank in range(1, count + 1)]
    largest = most if full else min(most, max(-(-total // count), total * loads[0] // sum(loads)))
    least = 1 if total - largest >= count - 1 else 0
    given, spare = [largest] + [least] * (count - 1), total - largest - least * (count - 1)
    while spare > 0:
        candidates = [i for i in range(1, count) if given[i] < largest] or [i for i in range(1, count) if given[i] < most]
        pool, remaining = sum([loads[i] for i in candidates]), spare
        for i in candidates:
            extra = min(most - given[i], max(1, remaining * loads[i] // pool), spare)
            given[i] = given[i] + extra
            spare = spare - extra
    return np.array(given)


def normal_values(stream_key, extent, scale, bound, pieces=(), kind=jnp.bfloat16):
    level = block_scale(stream_key, extent, pieces, -0.22, 0.18) if pieces else 1.0
    drawn = jax.random.normal(stream_key, extent, jnp.float32) * scale * level
    return jnp.minimum(jnp.maximum(drawn, -bound), bound).astype(kind)


def setup_inputs(seed: int = 0, part: int = 0) -> dict:
    splits = jax.random.split(jax.random.key(seed), 12)
    part_splits = jax.random.split(jax.random.fold_in(splits[11], part), 12)
    queries = draw_queries(jax.random.fold_in(jax.random.fold_in(splits[11], part), 71), part)
    keys = draw_keys(jax.random.fold_in(jax.random.fold_in(splits[11], part), 71), part)
    values = normal_values(part_splits[2], (CTX_LEN, KV_HEADS * HD), 1.0, 6.0, ((0, 4), (1, 4)))
    out_weight = normal_values(splits[3], (HEADS * HD, D), (HEADS * HD) ** -0.5, 0.125, ((0, 4), (1, 4)))
    residual = normal_values(part_splits[4], (NEW, D), 0.3, 2.0, ((0, 4), (1, 4)))
    router = normal_values(splits[5], (D, EXPERTS), D ** -0.5, 0.09375, (), jnp.float32)
    routes_keys = jax.random.split(jax.random.fold_in(part_splits[6], 1), NEW // TOK_DEV)
    routes_turns = jax.random.permutation(jax.random.fold_in(part_splits[6], 3), NEW // TOK_DEV)
    routes = jax.vmap(lambda own, number: assign_block(jax.random.fold_in(part_splits[6], 2), own, number, TOK_DEV, EXPERTS, 2, MOST, 2))(routes_keys, routes_turns).reshape((NEW, 2))
    order = jax.random.permutation(part_splits[7], NEW).astype(jnp.int32)
    expert_gate = normal_values(splits[8], (EXPERTS, D, FF), D ** -0.5, 0.09375, ((0, 4), (2, 4)))
    expert_up = normal_values(splits[9], (EXPERTS, D, FF), D ** -0.5, 0.09375, ((0, 4), (2, 4)))
    expert_down = normal_values(splits[10], (EXPERTS, FF, D), FF ** -0.5, 0.0625, ((0, 4), (1, 4)))
    return dict(queries=queries, keys=keys, values=values, out_weight=out_weight, residual=residual, router=router, routes=routes, order=order, expert_gate=expert_gate, expert_up=expert_up, expert_down=expert_down)


def reference(queries, keys, values, out_weight, residual, router, routes, order, expert_gate, expert_up, expert_down):
    score_scale = 1.0 / math.sqrt(HD)
    visible_end = (CTX_LEN - NEW + order).astype(jnp.int32)
    positions = jnp.arange(CTX_LEN, dtype=jnp.int32)
    visible = positions[None, :] <= visible_end[:, None]

    def one_head(index):
        group = (index // QPK).astype(jnp.int32)
        query = lax.dynamic_slice_in_dim(queries, (index * HD).astype(jnp.int32), HD, 1)
        key_head = lax.dynamic_slice_in_dim(keys, (group * HD).astype(jnp.int32), HD, 1)
        value_head = lax.dynamic_slice_in_dim(values, (group * HD).astype(jnp.int32), HD, 1)
        score = jnp.dot(query, key_head.T, preferred_element_type=jnp.float32) * score_scale
        score = jnp.where(visible, score, -1e+30)
        highest = lax.optimization_barrier(jnp.max(score, axis=1, keepdims=True))
        weight = jnp.where(visible, jnp.exp(score - highest), 0.0)
        total = lax.optimization_barrier(jnp.sum(weight, axis=1))
        summed = jnp.dot(weight.astype(jnp.bfloat16), value_head, preferred_element_type=jnp.float32)
        return (summed / total[:, None]).astype(jnp.bfloat16)
    heads_out = lax.map(one_head, jnp.arange(HEADS, dtype=jnp.int32))
    attended = jnp.transpose(heads_out, (1, 0, 2)).reshape(NEW, HEADS * HD)
    stream = jnp.dot(attended, out_weight, preferred_element_type=jnp.float32) + residual.astype(jnp.float32)
    normed = (stream * lax.rsqrt(lax.optimization_barrier(jnp.mean(stream * stream, axis=1, keepdims=True)) + 1e-05)).astype(jnp.bfloat16)
    logits = jnp.dot(normed.astype(jnp.float32), router, precision=lax.Precision.HIGHEST)
    chosen = jnp.take_along_axis(logits, routes, axis=1)
    first = jax.nn.sigmoid(chosen[:, 0] - chosen[:, 1])
    second = jax.nn.sigmoid(chosen[:, 1] - chosen[:, 0])
    gates = jnp.stack([first, second], axis=1)
    group_width = FF // N_CTX
    capacity = N_CTX * MOST

    def expert_step(index, accumulated):
        named = routes == index
        used = jnp.any(named, axis=1)
        weight_rows = lax.optimization_barrier(jnp.sum(jnp.where(named, gates, 0.0), axis=1))
        picked = jnp.argsort(1 - used.astype(jnp.int32), stable=True)[:capacity].astype(jnp.int32)
        rows = normed[picked]
        gate_proj = jnp.dot(rows, expert_gate[index], preferred_element_type=jnp.float32)
        up_proj = jnp.dot(rows, expert_up[index], preferred_element_type=jnp.float32)
        act = (jax.nn.silu(gate_proj) * up_proj).astype(jnp.bfloat16)
        down_here = expert_down[index]

        def add_group(group, summed):
            start = (group * group_width).astype(jnp.int32)
            piece = lax.dynamic_slice_in_dim(act, start, group_width, 1)
            block = lax.dynamic_slice_in_dim(down_here, start, group_width, 0)
            part = jnp.dot(piece, block, preferred_element_type=jnp.float32).astype(jnp.bfloat16)
            return summed + lax.optimization_barrier(part).astype(jnp.float32)
        summed = lax.fori_loop(0, N_CTX, add_group, jnp.zeros((capacity, D), jnp.float32))
        return accumulated.at[picked].add(weight_rows[picked][:, None] * summed)
    mixture = lax.fori_loop(0, EXPERTS, expert_step, jnp.zeros((NEW, D), jnp.float32))
    return (stream + mixture).astype(jnp.bfloat16)
```

```python
import math

import jax
import jax.numpy as jnp
from jax import lax
from jax.sharding import PartitionSpec as P


def rotation(count, step):
    return [(i, (i + step) % count) for i in range(count)]


def gather_rotated(block, count):
    return [block] + [lax.ppermute(block, "ctx", rotation(count, k)) for k in range(1, count)]


def picker_of(named, capacity):
    slot = jnp.cumsum(named.astype(jnp.int32)) - 1
    places = jnp.arange(capacity, dtype=jnp.int32)
    return (slot[None, :] == places[:, None]) & named[None, :]


def local(
    queries,
    keys,
    values,
    out_weight,
    residual,
    router,
    routes,
    order,
    expert_gate,
    expert_up,
    expert_down,
):
    bf16, f32 = jnp.bfloat16, jnp.float32
    tok = queries.shape[0]
    head_dim = keys.shape[1]
    heads = queries.shape[1] // head_dim
    span = keys.shape[0]
    ctx_count = lax.axis_size("ctx")
    exp_count = lax.axis_size("exp")
    c = lax.axis_index("ctx")
    e = lax.axis_index("exp")
    width = out_weight.shape[1]
    features = width * ctx_count
    capacity = tok // 2
    per_share = ctx_count // exp_count
    levels = exp_count.bit_length() - 1

    routes_all = gather_rotated(routes, ctx_count)
    routes_stacked = jnp.stack(routes_all)
    pieces = residual.reshape(tok, per_share, width)
    residual_blocks = []
    for t in range(per_share):
        perm = []
        for ci in range(ctx_count):
            for ei in range(exp_count):
                to = (ei * per_share + (t + ci) % per_share, ci // per_share)
                perm.append((ci * exp_count + ei, to[0] * exp_count + to[1]))
        piece = lax.dynamic_index_in_dim(pieces, (t + c) % per_share, 1, keepdims=False)
        residual_blocks.append(lax.ppermute(piece, ("ctx", "exp"), perm))
    if per_share > 1:
        stacked = jnp.stack(residual_blocks)
        residual_blocks = [
            lax.dynamic_index_in_dim(stacked, (c - j) % per_share, 0, keepdims=False)
            for j in range(per_share)
        ]

    visible_end = span * ctx_count - tok * ctx_count + order
    keys_all = jnp.concatenate(gather_rotated(keys, ctx_count))
    values_all = jnp.concatenate(gather_rotated(values, ctx_count))
    positions = jnp.concatenate(
        [((c - k) % ctx_count) * span + jnp.arange(span, dtype=jnp.int32) for k in range(ctx_count)]
    )
    query_blocks = queries.reshape(tok, heads, head_dim)
    score = jnp.einsum(
        "tqd,jd->qtj", query_blocks, keys_all, preferred_element_type=f32
    ) * (1.0 / math.sqrt(head_dim))
    visible = positions[None, None, :] <= visible_end[None, :, None]
    score = jnp.where(visible, score, -1e30)
    highest = jnp.max(score, axis=2, keepdims=True)
    weight = jnp.where(visible, jnp.exp(score - highest), 0.0)
    total = jnp.sum(weight, axis=2)
    summed = jnp.einsum(
        "qtj,jd->tqd", weight.astype(bf16), values_all, preferred_element_type=f32
    )
    attended = (summed / total.T[:, :, None]).astype(bf16).reshape(tok, heads * head_dim)

    attended_all = jnp.stack(gather_rotated(attended, ctx_count))

    def share_of(index):
        rows = [
            lax.dynamic_index_in_dim(
                attended_all, (c - (index * per_share + j)) % ctx_count, 0, keepdims=False
            )
            for j in range(per_share)
        ]
        return jnp.concatenate(rows)

    low = e % 2
    half = exp_count // 2
    away = jnp.concatenate([share_of(1 - low + 2 * i) for i in range(half)])
    near = jnp.concatenate([share_of(low + 2 * i) for i in range(half)])
    sent = jnp.dot(away, out_weight, preferred_element_type=f32).astype(bf16)
    came = lax.ppermute(sent, "exp", [(i, i ^ 1) for i in range(exp_count)])
    acc = jnp.dot(near, out_weight, preferred_element_type=f32) + came.astype(f32)
    rows = per_share * tok
    for level in range(1, levels):
        bit = (e >> level) % 2
        half = half // 2
        acc = acc.reshape(half, 2, rows, width)
        sent = lax.dynamic_index_in_dim(acc, 1 - bit, 1, keepdims=False).astype(bf16)
        came = lax.ppermute(sent, "exp", [(i, i ^ (1 << level)) for i in range(exp_count)])
        acc = lax.dynamic_index_in_dim(acc, bit, 1, keepdims=False) + came.astype(f32)
    stream = acc.reshape(per_share, tok, width) + jnp.stack(residual_blocks).astype(f32)
    stream = stream.astype(bf16)

    pickers = []
    for k in range(exp_count):
        for j in range(per_share):
            block = lax.dynamic_index_in_dim(
                routes_stacked, (c - (e * per_share + j)) % ctx_count, 0, keepdims=False
            )
            pickers.append(picker_of(jnp.any(block == (e ^ k), axis=1), capacity).astype(bf16))
    turns = sorted(range(ctx_count), key=lambda k: min(k, ctx_count - k))
    chunks = {}
    for k in turns:
        chunk = lax.ppermute(stream, "ctx", rotation(ctx_count, k)) if k else stream
        pieces = []
        for m in range(exp_count):
            picked = [
                jnp.dot(pickers[m * per_share + j], chunk[j], preferred_element_type=f32)
                for j in range(per_share)
            ]
            piece = jnp.concatenate(picked).astype(bf16)
            if m:
                piece = lax.ppermute(piece, "exp", [(i, i ^ m) for i in range(exp_count)])
            pieces.append(piece)
        chunks[k] = jnp.concatenate(pieces)

    gate_here, up_here, down_here = expert_gate[0], expert_up[0], expert_down[0]
    gate_proj = up_proj = squares = logits = 0.0
    for k in turns:
        chunk = chunks[k]
        start = ((c - k) % ctx_count) * width
        gate_rows = lax.dynamic_slice_in_dim(gate_here, start, width, 0)
        up_rows = lax.dynamic_slice_in_dim(up_here, start, width, 0)
        router_rows = lax.dynamic_slice_in_dim(router, start, width, 0)
        gate_proj += jnp.dot(chunk, gate_rows, preferred_element_type=f32)
        up_proj += jnp.dot(chunk, up_rows, preferred_element_type=f32)
        squares += jnp.sum(jnp.square(chunk.astype(f32)), axis=1, keepdims=True)
        logits += jnp.dot(chunk.astype(f32), router_rows, precision=lax.Precision.HIGHEST)
        gate_proj, up_proj, squares, logits = lax.optimization_barrier(
            (gate_proj, up_proj, squares, logits)
        )
    scale = lax.rsqrt(squares / features + 1e-05)
    act = (jax.nn.silu(gate_proj * scale) * (up_proj * scale)).astype(bf16)
    logits = logits * scale

    def rows_of(array, block):
        slot = ((e ^ (block // per_share)) * per_share + block % per_share) * capacity
        return lax.dynamic_slice_in_dim(array, slot, capacity, 0)

    own_rows = jnp.stack([rows_of(chunks[k], c) for k in range(ctx_count)])
    stream_rows = jnp.concatenate(
        [
            lax.dynamic_index_in_dim(own_rows, (c - a) % ctx_count, 0, keepdims=False)
            for a in range(ctx_count)
        ],
        axis=1,
    )

    experts = jnp.arange(router.shape[1], dtype=jnp.int32)
    mine = (experts == e).astype(f32)[None, :]
    own_share = tok // exp_count

    def contribution(k):
        block = (c + k) % ctx_count
        block_routes = routes_all[-k % ctx_count]
        picker = picker_of(jnp.any(block_routes == e, axis=1), capacity).astype(f32)
        other = jnp.sum(jnp.where(block_routes == e, 0, block_routes), axis=1)
        other_slot = jnp.dot(picker, (other[:, None] == experts[None, :]).astype(f32))
        gate = jax.nn.sigmoid(
            jnp.sum(rows_of(logits, block) * (mine - other_slot), axis=1, keepdims=True)
        )
        gives = gate * jnp.dot(rows_of(act, block), down_here, preferred_element_type=f32)
        if k == 0:
            gives += 0.5 * stream_rows.astype(f32)
        gives = gives.astype(bf16)
        spread = picker.T.astype(bf16).reshape(exp_count // 2, 2, own_share, capacity)

        def spread_rows(bit):
            pick = lax.dynamic_index_in_dim(spread, bit, 1, keepdims=False)
            return jnp.dot(
                pick.reshape(tok // 2, capacity), gives, preferred_element_type=f32
            )

        sent = spread_rows(1 - low).astype(bf16)
        came = lax.ppermute(sent, "exp", [(i, i ^ 1) for i in range(exp_count)])
        acc = spread_rows(low) + came.astype(f32)
        half = exp_count // 2
        for level in range(1, levels):
            bit = (e >> level) % 2
            half = half // 2
            acc = acc.reshape(half, 2, own_share, features)
            sent = lax.dynamic_index_in_dim(acc, 1 - bit, 1, keepdims=False).astype(bf16)
            came = lax.ppermute(sent, "exp", [(i, i ^ (1 << level)) for i in range(exp_count)])
            acc = lax.dynamic_index_in_dim(acc, bit, 1, keepdims=False) + came.astype(f32)
        return acc.reshape(own_share, features)

    output = 0.0
    for k in reversed(turns):
        part = contribution(k)
        if k:
            part = lax.ppermute(part.astype(bf16), "ctx", rotation(ctx_count, k)).astype(f32)
        output += part
    return output.astype(bf16)


def solution(mesh):
    return jax.shard_map(
        local,
        mesh=mesh,
        in_specs=(
            P(("groups", "ctx"), "exp"),
            P(("groups", "ctx"), "exp"),
            P(("groups", "ctx"), "exp"),
            P("exp", "ctx"),
            P(("groups", "ctx"), "exp"),
            P(),
            P(("groups", "ctx"), None),
            P(("groups", "ctx")),
            P("exp", None, "ctx"),
            P("exp", None, "ctx"),
            P("exp", "ctx", None),
        ),
        out_specs=P(("groups", "ctx", "exp"), None),
        check_vma=False,
    )
```

```python
import math

import jax
import jax.numpy as jnp
from jax import lax
from jax.sharding import PartitionSpec as P


def rotation(count, step):
    return [(i, (i + step) % count) for i in range(count)]


def gather_rotated(block, count):
    return [block] + [lax.ppermute(block, "ctx", rotation(count, k)) for k in range(1, count)]


def picker_of(named, capacity):
    slot = jnp.cumsum(named.astype(jnp.int32)) - 1
    places = jnp.arange(capacity, dtype=jnp.int32)
    return (slot[None, :] == places[:, None]) & named[None, :]


def local(
    queries,
    keys,
    values,
    out_weight,
    residual,
    router,
    routes,
    order,
    expert_gate,
    expert_up,
    expert_down,
):
    bf16, f32 = jnp.bfloat16, jnp.float32
    tok = queries.shape[0]
    head_dim = keys.shape[1]
    heads = queries.shape[1] // head_dim
    span = keys.shape[0]
    ctx_count = lax.axis_size("ctx")
    exp_count = lax.axis_size("exp")
    c = lax.axis_index("ctx")
    e = lax.axis_index("exp")
    width = out_weight.shape[1]
    features = width * ctx_count
    capacity = tok // 2
    per_share = ctx_count // exp_count
    levels = exp_count.bit_length() - 1

    routes_all = gather_rotated(routes, ctx_count)
    routes_stacked = jnp.stack(routes_all)
    pieces = residual.reshape(tok, per_share, width)
    residual_blocks = []
    for t in range(per_share):
        perm = []
        for ci in range(ctx_count):
            for ei in range(exp_count):
                to = (ei * per_share + (t + ci) % per_share, ci // per_share)
                perm.append((ci * exp_count + ei, to[0] * exp_count + to[1]))
        piece = lax.dynamic_index_in_dim(pieces, (t + c) % per_share, 1, keepdims=False)
        residual_blocks.append(lax.ppermute(piece, ("ctx", "exp"), perm))
    if per_share > 1:
        stacked = jnp.stack(residual_blocks)
        residual_blocks = [
            lax.dynamic_index_in_dim(stacked, (c - j) % per_share, 0, keepdims=False)
            for j in range(per_share)
        ]

    visible_end = span * ctx_count - tok * ctx_count + order
    keys_all = jnp.concatenate(gather_rotated(keys, ctx_count))
    values_all = jnp.concatenate(gather_rotated(values, ctx_count))
    keys_all = lax.optimization_barrier(keys_all)
    positions = jnp.concatenate(
        [((c - k) % ctx_count) * span + jnp.arange(span, dtype=jnp.int32) for k in range(ctx_count)]
    )
    query_blocks = queries.reshape(tok, heads, head_dim)
    score = jnp.einsum(
        "tqd,jd->qtj", query_blocks, keys_all, preferred_element_type=f32
    ) * (1.0 / math.sqrt(head_dim))
    visible = lax.optimization_barrier(positions[None, :] <= visible_end[:, None])[None]
    score = jnp.where(visible, score, -1e30)
    highest = jnp.max(score, axis=2, keepdims=True)
    weight = jnp.where(visible, jnp.exp(score - highest), 0.0)
    total = jnp.sum(weight, axis=2)
    summed = jnp.einsum(
        "qtj,jd->tqd", weight.astype(bf16), values_all, preferred_element_type=f32
    )
    attended = (summed / total.T[:, :, None]).astype(bf16).reshape(tok, heads * head_dim)

    attended_all = jnp.stack(gather_rotated(attended, ctx_count))

    def share_of(index):
        rows = [
            lax.dynamic_index_in_dim(
                attended_all, (c - (index * per_share + j)) % ctx_count, 0, keepdims=False
            )
            for j in range(per_share)
        ]
        return jnp.concatenate(rows)

    low = e % 2
    half = exp_count // 2
    away = jnp.concatenate([share_of(1 - low + 2 * i) for i in range(half)])
    near = jnp.concatenate([share_of(low + 2 * i) for i in range(half)])
    sent = jnp.dot(away, out_weight, preferred_element_type=f32).astype(bf16)
    came = lax.ppermute(sent, "exp", [(i, i ^ 1) for i in range(exp_count)])
    acc = jnp.dot(near, out_weight, preferred_element_type=f32) + came.astype(f32)
    rows = per_share * tok
    for level in range(1, levels):
        bit = (e >> level) % 2
        half = half // 2
        acc = acc.reshape(half, 2, rows, width)
        sent = lax.dynamic_index_in_dim(acc, 1 - bit, 1, keepdims=False).astype(bf16)
        came = lax.ppermute(sent, "exp", [(i, i ^ (1 << level)) for i in range(exp_count)])
        acc = lax.dynamic_index_in_dim(acc, bit, 1, keepdims=False) + came.astype(f32)
    stream = acc.reshape(per_share, tok, width) + jnp.stack(residual_blocks).astype(f32)
    stream = stream.astype(bf16)

    pickers = []
    for k in range(exp_count):
        for j in range(per_share):
            block = lax.dynamic_index_in_dim(
                routes_stacked, (c - (e * per_share + j)) % ctx_count, 0, keepdims=False
            )
            pickers.append(picker_of(jnp.any(block == (e ^ k), axis=1), capacity).astype(bf16))
    pickers = lax.optimization_barrier(pickers)
    turns = sorted(range(ctx_count), key=lambda k: min(k, ctx_count - k))
    chunks = {}
    for k in turns:
        chunk = lax.ppermute(stream, "ctx", rotation(ctx_count, k)) if k else stream
        pieces = []
        for m in range(exp_count):
            picked = [
                jnp.dot(pickers[m * per_share + j], chunk[j], preferred_element_type=f32)
                for j in range(per_share)
            ]
            piece = jnp.concatenate(picked).astype(bf16)
            if m:
                piece = lax.ppermute(piece, "exp", [(i, i ^ m) for i in range(exp_count)])
            pieces.append(piece)
        chunks[k] = jnp.concatenate(pieces)

    gate_here, up_here, down_here = expert_gate[0], expert_up[0], expert_down[0]
    gate_proj = up_proj = squares = logits = 0.0
    for k in turns:
        chunk = chunks[k]
        start = ((c - k) % ctx_count) * width
        gate_rows = lax.dynamic_slice_in_dim(gate_here, start, width, 0)
        up_rows = lax.dynamic_slice_in_dim(up_here, start, width, 0)
        router_rows = lax.dynamic_slice_in_dim(router, start, width, 0)
        gate_proj += jnp.dot(chunk, gate_rows, preferred_element_type=f32)
        up_proj += jnp.dot(chunk, up_rows, preferred_element_type=f32)
        squares += jnp.sum(jnp.square(chunk.astype(f32)), axis=1, keepdims=True)
        logits += jnp.dot(chunk.astype(f32), router_rows, precision=lax.Precision.HIGHEST)
        gate_proj, up_proj, squares, logits = lax.optimization_barrier(
            (gate_proj, up_proj, squares, logits)
        )
    scale = lax.rsqrt(squares / features + 1e-05)
    act = (jax.nn.silu(gate_proj * scale) * (up_proj * scale)).astype(bf16)
    logits = logits * scale

    def rows_of(array, block):
        slot = ((e ^ (block // per_share)) * per_share + block % per_share) * capacity
        return lax.dynamic_slice_in_dim(array, slot, capacity, 0)

    own_rows = jnp.stack([rows_of(chunks[k], c) for k in range(ctx_count)])
    stream_rows = jnp.concatenate(
        [
            lax.dynamic_index_in_dim(own_rows, (c - a) % ctx_count, 0, keepdims=False)
            for a in range(ctx_count)
        ],
        axis=1,
    )

    experts = jnp.arange(router.shape[1], dtype=jnp.int32)
    mine = (experts == e).astype(f32)[None, :]
    own_share = tok // exp_count

    def contribution(k, gives):
        block = (c + k) % ctx_count
        block_routes = routes_all[-k % ctx_count]
        picker = picker_of(jnp.any(block_routes == e, axis=1), capacity).astype(f32)
        other = jnp.sum(jnp.where(block_routes == e, 0, block_routes), axis=1)
        other_slot = jnp.dot(picker, (other[:, None] == experts[None, :]).astype(f32))
        gate = jax.nn.sigmoid(
            jnp.sum(rows_of(logits, block) * (mine - other_slot), axis=1, keepdims=True)
        )
        gives *= gate
        if k == 0:
            gives += 0.5 * stream_rows.astype(f32)
        gives = gives.astype(bf16)
        spread = picker.T.astype(bf16).reshape(exp_count // 2, 2, own_share, capacity)

        def spread_rows(bit):
            pick = lax.dynamic_index_in_dim(spread, bit, 1, keepdims=False)
            return jnp.dot(
                pick.reshape(tok // 2, capacity), gives, preferred_element_type=f32
            )

        sent = spread_rows(1 - low).astype(bf16)
        came = lax.ppermute(sent, "exp", [(i, i ^ 1) for i in range(exp_count)])
        first = came
        acc = spread_rows(low) + came.astype(f32)
        half = exp_count // 2
        for level in range(1, levels):
            bit = (e >> level) % 2
            half = half // 2
            acc = acc.reshape(half, 2, own_share, features)
            sent = lax.dynamic_index_in_dim(acc, 1 - bit, 1, keepdims=False).astype(bf16)
            came = lax.ppermute(sent, "exp", [(i, i ^ (1 << level)) for i in range(exp_count)])
            acc = lax.dynamic_index_in_dim(acc, bit, 1, keepdims=False) + came.astype(f32)
        return acc.reshape(own_share, features), first

    direct = [k for k in (1,) if k < ctx_count]
    others = [k for k in reversed(turns) if k and k not in direct]
    added, output, after = 0.0, 0.0, ()
    for k in direct:
        part = jnp.dot(rows_of(act, (c + k) % ctx_count), down_here, preferred_element_type=f32)
        part = part.astype(bf16)
        after += (part,)
        added += lax.ppermute(part, "ctx", rotation(ctx_count, k)).astype(f32)
    for k in others:
        rows = rows_of(lax.optimization_barrier((act, after))[0], (c + k) % ctx_count)
        gives = jnp.dot(rows, down_here, preferred_element_type=f32)
        part, after = contribution(k, gives)
        part = part.astype(bf16)
        output += lax.ppermute(part, "ctx", rotation(ctx_count, k)).astype(f32)
    rows = rows_of(lax.optimization_barrier((act, after))[0], c)
    gives = jnp.dot(rows, down_here, preferred_element_type=f32)
    gives = lax.optimization_barrier(gives)
    part, _ = contribution(0, gives + added)
    return (output + part).astype(bf16)


def solution(mesh):
    return jax.shard_map(
        local,
        mesh=mesh,
        in_specs=(
            P(("groups", "ctx"), "exp"),
            P(("groups", "ctx"), "exp"),
            P(("groups", "ctx"), "exp"),
            P("exp", "ctx"),
            P(("groups", "ctx"), "exp"),
            P(),
            P(("groups", "ctx"), None),
            P(("groups", "ctx")),
            P("exp", None, "ctx"),
            P("exp", None, "ctx"),
            P("exp", "ctx", None),
        ),
        out_specs=P(("groups", "ctx", "exp"), None),
        check_vma=False,
    )
```

```python
import math

import jax
import jax.numpy as jnp
from jax import lax
from jax.sharding import PartitionSpec as P


def rotation(count, step):
    return [(i, (i + step) % count) for i in range(count)]


def gather_rotated(block, count):
    return [block] + [lax.ppermute(block, "ctx", rotation(count, k)) for k in range(1, count)]


def picker_of(named, capacity):
    slot = jnp.cumsum(named.astype(jnp.int32)) - 1
    places = jnp.arange(capacity, dtype=jnp.int32)
    return (slot[None, :] == places[:, None]) & named[None, :]


def local(
    queries,
    keys,
    values,
    out_weight,
    residual,
    router,
    routes,
    order,
    expert_gate,
    expert_up,
    expert_down,
):
    bf16, f32 = jnp.bfloat16, jnp.float32
    tok = queries.shape[0]
    head_dim = keys.shape[1]
    heads = queries.shape[1] // head_dim
    span = keys.shape[0]
    ctx_count = lax.axis_size("ctx")
    exp_count = lax.axis_size("exp")
    c = lax.axis_index("ctx")
    e = lax.axis_index("exp")
    width = out_weight.shape[1]
    features = width * ctx_count
    capacity = tok // 2
    per_share = ctx_count // exp_count
    levels = exp_count.bit_length() - 1

    routes_all = gather_rotated(routes, ctx_count)
    routes_stacked = jnp.stack(routes_all)
    pieces = residual.reshape(tok, per_share, width)
    residual_blocks = []
    for t in range(per_share):
        perm = []
        for ci in range(ctx_count):
            for ei in range(exp_count):
                to = (ei * per_share + (t + ci) % per_share, ci // per_share)
                perm.append((ci * exp_count + ei, to[0] * exp_count + to[1]))
        piece = lax.dynamic_index_in_dim(pieces, (t + c) % per_share, 1, keepdims=False)
        residual_blocks.append(lax.ppermute(piece, ("ctx", "exp"), perm))
    if per_share > 1:
        stacked = jnp.stack(residual_blocks)
        residual_blocks = [
            lax.dynamic_index_in_dim(stacked, (c - j) % per_share, 0, keepdims=False)
            for j in range(per_share)
        ]

    visible_end = span * ctx_count - tok * ctx_count + order
    keys_all = jnp.concatenate(gather_rotated(keys, ctx_count))
    values_all = jnp.concatenate(gather_rotated(values, ctx_count))
    keys_all = lax.optimization_barrier(keys_all)
    positions = jnp.concatenate(
        [((c - k) % ctx_count) * span + jnp.arange(span, dtype=jnp.int32) for k in range(ctx_count)]
    )
    query_blocks = queries.reshape(tok, heads, head_dim)
    score = jnp.einsum(
        "tqd,jd->qtj", query_blocks, keys_all, preferred_element_type=f32
    ) * (1.0 / math.sqrt(head_dim))
    visible = lax.optimization_barrier(positions[None, :] <= visible_end[:, None])[None]
    score = jnp.where(visible, score, -1e30)
    highest = jnp.max(score, axis=2, keepdims=True)
    weight = jnp.where(visible, jnp.exp(score - highest), 0.0)
    total = jnp.sum(weight, axis=2)
    summed = jnp.einsum(
        "qtj,jd->tqd", weight.astype(bf16), values_all, preferred_element_type=f32
    )
    attended = (summed / total.T[:, :, None]).astype(bf16).reshape(tok, heads * head_dim)

    attended_all = jnp.stack(gather_rotated(attended, ctx_count))

    def share_of(index):
        rows = [
            lax.dynamic_index_in_dim(
                attended_all, (c - (index * per_share + j)) % ctx_count, 0, keepdims=False
            )
            for j in range(per_share)
        ]
        return jnp.concatenate(rows)

    low = e % 2
    half = exp_count // 2
    away = jnp.concatenate([share_of(1 - low + 2 * i) for i in range(half)])
    near = jnp.concatenate([share_of(low + 2 * i) for i in range(half)])
    sent = jnp.dot(away, out_weight, preferred_element_type=f32).astype(bf16)
    came = lax.ppermute(sent, "exp", [(i, i ^ 1) for i in range(exp_count)])
    acc = jnp.dot(near, out_weight, preferred_element_type=f32) + came.astype(f32)
    rows = per_share * tok
    for level in range(1, levels):
        bit = (e >> level) % 2
        half = half // 2
        acc = acc.reshape(half, 2, rows, width)
        sent = lax.dynamic_index_in_dim(acc, 1 - bit, 1, keepdims=False).astype(bf16)
        came = lax.ppermute(sent, "exp", [(i, i ^ (1 << level)) for i in range(exp_count)])
        acc = lax.dynamic_index_in_dim(acc, bit, 1, keepdims=False) + came.astype(f32)
    stream = acc.reshape(per_share, tok, width) + jnp.stack(residual_blocks).astype(f32)
    stream = stream.astype(bf16)

    pickers = []
    for k in range(exp_count):
        for j in range(per_share):
            block = lax.dynamic_index_in_dim(
                routes_stacked, (c - (e * per_share + j)) % ctx_count, 0, keepdims=False
            )
            pickers.append(picker_of(jnp.any(block == (e ^ k), axis=1), capacity).astype(bf16))
    pickers = lax.optimization_barrier(pickers)
    turns = sorted(range(ctx_count), key=lambda k: min(k, ctx_count - k))
    chunks, moved = {}, {}
    for k in turns:
        if k == turns[-1] and ctx_count > 2:
            chunk = lax.optimization_barrier((stream, moved[turns[0]][exp_count // 2]))[0]
        else:
            chunk = stream
        if k:
            chunk = lax.ppermute(chunk, "ctx", rotation(ctx_count, k))
        pieces = []
        for m in range(exp_count):
            picked = [
                jnp.dot(pickers[m * per_share + j], chunk[j], preferred_element_type=f32)
                for j in range(per_share)
            ]
            piece = jnp.concatenate(picked).astype(bf16)
            if m:
                piece = lax.ppermute(piece, "exp", [(i, i ^ m) for i in range(exp_count)])
            pieces.append(piece)
        moved[k] = pieces
        chunks[k] = jnp.concatenate(pieces)

    gate_here, up_here, down_here = expert_gate[0], expert_up[0], expert_down[0]
    gate_proj = up_proj = squares = logits = 0.0
    for k in turns:
        chunk = chunks[k]
        start = ((c - k) % ctx_count) * width
        gate_rows = lax.dynamic_slice_in_dim(gate_here, start, width, 0)
        up_rows = lax.dynamic_slice_in_dim(up_here, start, width, 0)
        router_rows = lax.dynamic_slice_in_dim(router, start, width, 0)
        gate_proj += jnp.dot(chunk, gate_rows, preferred_element_type=f32)
        up_proj += jnp.dot(chunk, up_rows, preferred_element_type=f32)
        squares += jnp.sum(jnp.square(chunk.astype(f32)), axis=1, keepdims=True)
        logits += jnp.dot(chunk.astype(f32), router_rows, precision=lax.Precision.HIGHEST)
        gate_proj, up_proj, squares, logits = lax.optimization_barrier(
            (gate_proj, up_proj, squares, logits)
        )
    scale = lax.rsqrt(squares / features + 1e-05)
    act = (jax.nn.silu(gate_proj * scale) * (up_proj * scale)).astype(bf16)
    logits = logits * scale

    def rows_of(array, block):
        slot = ((e ^ (block // per_share)) * per_share + block % per_share) * capacity
        return lax.dynamic_slice_in_dim(array, slot, capacity, 0)

    own_rows = jnp.stack([rows_of(chunks[k], c) for k in range(ctx_count)])
    stream_rows = jnp.concatenate(
        [
            lax.dynamic_index_in_dim(own_rows, (c - a) % ctx_count, 0, keepdims=False)
            for a in range(ctx_count)
        ],
        axis=1,
    )

    experts = jnp.arange(router.shape[1], dtype=jnp.int32)
    mine = (experts == e).astype(f32)[None, :]
    own_share = tok // exp_count

    def contribution(k, gives):
        block = (c + k) % ctx_count
        block_routes = routes_all[-k % ctx_count]
        picker = picker_of(jnp.any(block_routes == e, axis=1), capacity).astype(f32)
        other = jnp.sum(jnp.where(block_routes == e, 0, block_routes), axis=1)
        other_slot = jnp.dot(picker, (other[:, None] == experts[None, :]).astype(f32))
        gate = jax.nn.sigmoid(
            jnp.sum(rows_of(logits, block) * (mine - other_slot), axis=1, keepdims=True)
        )
        gives *= gate
        if k == 0:
            gives += 0.5 * stream_rows.astype(f32)
        gives = gives.astype(bf16)
        spread = picker.T.astype(bf16).reshape(exp_count // 2, 2, own_share, capacity)

        def spread_rows(bit):
            pick = lax.dynamic_index_in_dim(spread, bit, 1, keepdims=False)
            return jnp.dot(
                pick.reshape(tok // 2, capacity), gives, preferred_element_type=f32
            )

        sent = spread_rows(1 - low).astype(bf16)
        came = lax.ppermute(sent, "exp", [(i, i ^ 1) for i in range(exp_count)])
        first = came
        acc = spread_rows(low) + came.astype(f32)
        half = exp_count // 2
        for level in range(1, levels):
            bit = (e >> level) % 2
            half = half // 2
            acc = acc.reshape(half, 2, own_share, features)
            sent = lax.dynamic_index_in_dim(acc, 1 - bit, 1, keepdims=False).astype(bf16)
            came = lax.ppermute(sent, "exp", [(i, i ^ (1 << level)) for i in range(exp_count)])
            acc = lax.dynamic_index_in_dim(acc, bit, 1, keepdims=False) + came.astype(f32)
        return acc.reshape(own_share, features), first

    direct = [k for k in (1,) if k < ctx_count]
    others = [k for k in reversed(turns) if k and k not in direct]
    added, output, after = 0.0, 0.0, ()
    for k in direct:
        part = jnp.dot(rows_of(act, (c + k) % ctx_count), down_here, preferred_element_type=f32)
        part = part.astype(bf16)
        after += (part,)
        added += lax.ppermute(part, "ctx", rotation(ctx_count, k)).astype(f32)
    for k in others:
        rows = rows_of(lax.optimization_barrier((act, after))[0], (c + k) % ctx_count)
        gives = jnp.dot(rows, down_here, preferred_element_type=f32)
        part, after = contribution(k, gives)
        part = part.astype(bf16)
        output += lax.ppermute(part, "ctx", rotation(ctx_count, k)).astype(f32)
    rows = rows_of(lax.optimization_barrier((act, after))[0], c)
    gives = jnp.dot(rows, down_here, preferred_element_type=f32)
    gives = lax.optimization_barrier(gives)
    part, _ = contribution(0, gives + added)
    return (output + part).astype(bf16)


def solution(mesh):
    return jax.shard_map(
        local,
        mesh=mesh,
        in_specs=(
            P(("groups", "ctx"), "exp"),
            P(("groups", "ctx"), "exp"),
            P(("groups", "ctx"), "exp"),
            P("exp", "ctx"),
            P(("groups", "ctx"), "exp"),
            P(),
            P(("groups", "ctx"), None),
            P(("groups", "ctx")),
            P("exp", None, "ctx"),
            P("exp", None, "ctx"),
            P("exp", "ctx", None),
        ),
        out_specs=P(("groups", "ctx", "exp"), None),
        check_vma=False,
    )
```

```python
import math

import jax
import jax.numpy as jnp
from jax import lax
from jax.sharding import PartitionSpec as P


def rotation(count, step):
    return [(i, (i + step) % count) for i in range(count)]


def gather_rotated(block, count):
    return [block] + [lax.ppermute(block, "ctx", rotation(count, k)) for k in range(1, count)]


def picker_of(named, capacity):
    slot = jnp.cumsum(named.astype(jnp.int32)) - 1
    places = jnp.arange(capacity, dtype=jnp.int32)
    return (slot[None, :] == places[:, None]) & named[None, :]


def local(
    queries,
    keys,
    values,
    out_weight,
    residual,
    router,
    routes,
    order,
    expert_gate,
    expert_up,
    expert_down,
):
    bf16, f32 = jnp.bfloat16, jnp.float32
    tok = queries.shape[0]
    head_dim = keys.shape[1]
    heads = queries.shape[1] // head_dim
    span = keys.shape[0]
    ctx_count = lax.axis_size("ctx")
    exp_count = lax.axis_size("exp")
    c = lax.axis_index("ctx")
    e = lax.axis_index("exp")
    width = out_weight.shape[1]
    features = width * ctx_count
    capacity = tok // 2
    per_share = ctx_count // exp_count
    levels = exp_count.bit_length() - 1

    routes_all = gather_rotated(routes, ctx_count)
    routes_stacked = jnp.stack(routes_all)
    pieces = residual.reshape(tok, per_share, width)
    residual_blocks = []
    for t in range(per_share):
        perm = []
        for ci in range(ctx_count):
            for ei in range(exp_count):
                to = (ei * per_share + (t + ci) % per_share, ci // per_share)
                perm.append((ci * exp_count + ei, to[0] * exp_count + to[1]))
        piece = lax.dynamic_index_in_dim(pieces, (t + c) % per_share, 1, keepdims=False)
        residual_blocks.append(lax.ppermute(piece, ("ctx", "exp"), perm))
    if per_share > 1:
        stacked = jnp.stack(residual_blocks)
        residual_blocks = [
            lax.dynamic_index_in_dim(stacked, (c - j) % per_share, 0, keepdims=False)
            for j in range(per_share)
        ]

    visible_end = span * ctx_count - tok * ctx_count + order
    keys_all = jnp.concatenate(gather_rotated(keys, ctx_count))
    values_all = jnp.concatenate(gather_rotated(values, ctx_count))
    keys_all = lax.optimization_barrier(keys_all)
    positions = jnp.concatenate(
        [((c - k) % ctx_count) * span + jnp.arange(span, dtype=jnp.int32) for k in range(ctx_count)]
    )
    query_blocks = queries.reshape(tok, heads, head_dim)
    score = jnp.einsum(
        "tqd,jd->qtj", query_blocks, keys_all, preferred_element_type=f32
    ) * (1.0 / math.sqrt(head_dim))
    visible = lax.optimization_barrier(positions[None, :] <= visible_end[:, None])[None]
    score = jnp.where(visible, score, -1e30)
    highest = jnp.max(score, axis=2, keepdims=True)
    weight = jnp.where(visible, jnp.exp(score - highest), 0.0)
    total = jnp.sum(weight, axis=2)
    summed = jnp.einsum(
        "qtj,jd->tqd", weight.astype(bf16), values_all, preferred_element_type=f32
    )
    attended = (summed / total.T[:, :, None]).astype(bf16).reshape(tok, heads * head_dim)

    attended_all = jnp.stack(gather_rotated(attended, ctx_count))

    def share_of(index):
        rows = [
            lax.dynamic_index_in_dim(
                attended_all, (c - (index * per_share + j)) % ctx_count, 0, keepdims=False
            )
            for j in range(per_share)
        ]
        return jnp.concatenate(rows)

    low = e % 2
    half = exp_count // 2
    away = jnp.concatenate([share_of(1 - low + 2 * i) for i in range(half)])
    near = jnp.concatenate([share_of(low + 2 * i) for i in range(half)])
    sent = jnp.dot(away, out_weight, preferred_element_type=f32).astype(bf16)
    came = lax.ppermute(sent, "exp", [(i, i ^ 1) for i in range(exp_count)])
    acc = jnp.dot(near, out_weight, preferred_element_type=f32) + came.astype(f32)
    rows = per_share * tok
    for level in range(1, levels):
        bit = (e >> level) % 2
        half = half // 2
        acc = acc.reshape(half, 2, rows, width)
        sent = lax.dynamic_index_in_dim(acc, 1 - bit, 1, keepdims=False).astype(bf16)
        came = lax.ppermute(sent, "exp", [(i, i ^ (1 << level)) for i in range(exp_count)])
        acc = lax.dynamic_index_in_dim(acc, bit, 1, keepdims=False) + came.astype(f32)
    stream = acc.reshape(per_share, tok, width) + jnp.stack(residual_blocks).astype(f32)
    stream = stream.astype(bf16)

    pickers = []
    for k in range(exp_count):
        for j in range(per_share):
            block = lax.dynamic_index_in_dim(
                routes_stacked, (c - (e * per_share + j)) % ctx_count, 0, keepdims=False
            )
            pickers.append(picker_of(jnp.any(block == (e ^ k), axis=1), capacity).astype(bf16))
    pickers = lax.optimization_barrier(pickers)
    turns = sorted(range(ctx_count), key=lambda k: min(k, ctx_count - k))
    chunks, moved = {}, {}
    for k in turns:
        if k == turns[-1] and ctx_count > 2:
            chunk = lax.optimization_barrier((stream, moved[turns[0]][exp_count // 2]))[0]
        else:
            chunk = stream
        if k:
            chunk = lax.ppermute(chunk, "ctx", rotation(ctx_count, k))
        pieces = []
        for m in range(exp_count):
            picked = [
                jnp.dot(pickers[m * per_share + j], chunk[j], preferred_element_type=f32)
                for j in range(per_share)
            ]
            piece = jnp.concatenate(picked).astype(bf16)
            if m:
                piece = lax.ppermute(piece, "exp", [(i, i ^ m) for i in range(exp_count)])
            pieces.append(piece)
        moved[k] = pieces
        chunks[k] = jnp.concatenate(pieces)

    gate_here, up_here, down_here = expert_gate[0], expert_up[0], expert_down[0]
    for k in turns[-1:]:
        chunks[k] = lax.optimization_barrier(chunks[k])
    gate_proj = up_proj = squares = logits = 0.0
    for k in turns:
        chunk = chunks[k]
        start = ((c - k) % ctx_count) * width
        gate_rows = lax.dynamic_slice_in_dim(gate_here, start, width, 0)
        up_rows = lax.dynamic_slice_in_dim(up_here, start, width, 0)
        router_rows = lax.dynamic_slice_in_dim(router, start, width, 0)
        gate_proj += jnp.dot(chunk, gate_rows, preferred_element_type=f32)
        up_proj += jnp.dot(chunk, up_rows, preferred_element_type=f32)
        squares += jnp.sum(jnp.square(chunk.astype(f32)), axis=1, keepdims=True)
        logits += jnp.dot(chunk.astype(f32), router_rows, precision=lax.Precision.HIGHEST)
        gate_proj, up_proj, squares, logits = lax.optimization_barrier(
            (gate_proj, up_proj, squares, logits)
        )
    scale = lax.rsqrt(squares / features + 1e-05)
    act = (jax.nn.silu(gate_proj * scale) * (up_proj * scale)).astype(bf16)
    logits = logits * scale

    def rows_of(array, block):
        slot = ((e ^ (block // per_share)) * per_share + block % per_share) * capacity
        return lax.dynamic_slice_in_dim(array, slot, capacity, 0)

    own_rows = jnp.stack([rows_of(chunks[k], c) for k in range(ctx_count)])
    stream_rows = jnp.concatenate(
        [
            lax.dynamic_index_in_dim(own_rows, (c - a) % ctx_count, 0, keepdims=False)
            for a in range(ctx_count)
        ],
        axis=1,
    )

    experts = jnp.arange(router.shape[1], dtype=jnp.int32)
    mine = (experts == e).astype(f32)[None, :]
    own_share = tok // exp_count

    def contribution(k, gives):
        block = (c + k) % ctx_count
        block_routes = routes_all[-k % ctx_count]
        picker = picker_of(jnp.any(block_routes == e, axis=1), capacity).astype(f32)
        other = jnp.sum(jnp.where(block_routes == e, 0, block_routes), axis=1)
        other_slot = jnp.dot(picker, (other[:, None] == experts[None, :]).astype(f32))
        gate = jax.nn.sigmoid(
            jnp.sum(rows_of(logits, block) * (mine - other_slot), axis=1, keepdims=True)
        )
        gives *= gate
        if k == 0:
            gives += 0.5 * stream_rows.astype(f32)
        gives = gives.astype(bf16)
        spread = picker.T.astype(bf16).reshape(exp_count // 2, 2, own_share, capacity)

        def spread_rows(bit):
            pick = lax.dynamic_index_in_dim(spread, bit, 1, keepdims=False)
            return jnp.dot(
                pick.reshape(tok // 2, capacity), gives, preferred_element_type=f32
            )

        sent = spread_rows(1 - low).astype(bf16)
        came = lax.ppermute(sent, "exp", [(i, i ^ 1) for i in range(exp_count)])
        first = came
        acc = spread_rows(low) + came.astype(f32)
        half = exp_count // 2
        for level in range(1, levels):
            bit = (e >> level) % 2
            half = half // 2
            acc = acc.reshape(half, 2, own_share, features)
            sent = lax.dynamic_index_in_dim(acc, 1 - bit, 1, keepdims=False).astype(bf16)
            came = lax.ppermute(sent, "exp", [(i, i ^ (1 << level)) for i in range(exp_count)])
            acc = lax.dynamic_index_in_dim(acc, bit, 1, keepdims=False) + came.astype(f32)
        return acc.reshape(own_share, features), first

    direct = [k for k in (1,) if k < ctx_count]
    others = [k for k in reversed(turns) if k and k not in direct]
    added, output, after = 0.0, 0.0, ()
    for k in direct:
        part = jnp.dot(rows_of(act, (c + k) % ctx_count), down_here, preferred_element_type=f32)
        part = part.astype(bf16)
        after += (part,)
        added += lax.ppermute(part, "ctx", rotation(ctx_count, k)).astype(f32)
    for k in others:
        rows = rows_of(lax.optimization_barrier((act, after))[0], (c + k) % ctx_count)
        gives = jnp.dot(rows, down_here, preferred_element_type=f32)
        part, after = contribution(k, gives)
        part = part.astype(bf16)
        output += lax.ppermute(part, "ctx", rotation(ctx_count, k)).astype(f32)
    rows = rows_of(lax.optimization_barrier((act, after))[0], c)
    gives = jnp.dot(rows, down_here, preferred_element_type=f32)
    gives = lax.optimization_barrier(gives)
    part, _ = contribution(0, gives + added)
    return (output + part).astype(bf16)


def solution(mesh):
    return jax.shard_map(
        local,
        mesh=mesh,
        in_specs=(
            P(("groups", "ctx"), "exp"),
            P(("groups", "ctx"), "exp"),
            P(("groups", "ctx"), "exp"),
            P("exp", "ctx"),
            P(("groups", "ctx"), "exp"),
            P(),
            P(("groups", "ctx"), None),
            P(("groups", "ctx")),
            P("exp", None, "ctx"),
            P("exp", None, "ctx"),
            P("exp", "ctx", None),
        ),
        out_specs=P(("groups", "ctx", "exp"), None),
        check_vma=False,
    )
```

```python
import math

import jax
import jax.numpy as jnp
from jax import lax
from jax.sharding import PartitionSpec as P


def rotation(count, step):
    return [(i, (i + step) % count) for i in range(count)]


def gather_rotated(block, count):
    return [block] + [lax.ppermute(block, "ctx", rotation(count, k)) for k in range(1, count)]


def picker_of(named, capacity):
    slot = jnp.cumsum(named.astype(jnp.int32)) - 1
    places = jnp.arange(capacity, dtype=jnp.int32)
    return (slot[None, :] == places[:, None]) & named[None, :]


def local(
    queries,
    keys,
    values,
    out_weight,
    residual,
    router,
    routes,
    order,
    expert_gate,
    expert_up,
    expert_down,
):
    bf16, f32 = jnp.bfloat16, jnp.float32
    tok = queries.shape[0]
    head_dim = keys.shape[1]
    heads = queries.shape[1] // head_dim
    span = keys.shape[0]
    ctx_count = lax.axis_size("ctx")
    exp_count = lax.axis_size("exp")
    c = lax.axis_index("ctx")
    e = lax.axis_index("exp")
    width = out_weight.shape[1]
    features = width * ctx_count
    capacity = tok // 2
    per_share = ctx_count // exp_count
    levels = exp_count.bit_length() - 1

    routes_all = gather_rotated(routes, ctx_count)
    routes_stacked = jnp.stack(routes_all)
    pieces = residual.reshape(tok, per_share, width)
    residual_blocks = []
    for t in range(per_share):
        perm = []
        for ci in range(ctx_count):
            for ei in range(exp_count):
                to = (ei * per_share + (t + ci) % per_share, ci // per_share)
                perm.append((ci * exp_count + ei, to[0] * exp_count + to[1]))
        piece = lax.dynamic_index_in_dim(pieces, (t + c) % per_share, 1, keepdims=False)
        residual_blocks.append(lax.ppermute(piece, ("ctx", "exp"), perm))
    if per_share > 1:
        stacked = jnp.stack(residual_blocks)
        residual_blocks = [
            lax.dynamic_index_in_dim(stacked, (c - j) % per_share, 0, keepdims=False)
            for j in range(per_share)
        ]

    visible_end = span * ctx_count - tok * ctx_count + order
    keys_all = jnp.concatenate(gather_rotated(keys, ctx_count))
    values_all = jnp.concatenate(gather_rotated(values, ctx_count))
    keys_all = lax.optimization_barrier(keys_all)
    positions = jnp.concatenate(
        [((c - k) % ctx_count) * span + jnp.arange(span, dtype=jnp.int32) for k in range(ctx_count)]
    )
    query_blocks = queries.reshape(tok, heads, head_dim)
    score = jnp.einsum(
        "tqd,jd->qtj", query_blocks, keys_all, preferred_element_type=f32
    ) * (1.0 / math.sqrt(head_dim))
    visible = lax.optimization_barrier(positions[None, :] <= visible_end[:, None])[None]
    score = jnp.where(visible, score, -1e30)
    highest = jnp.max(score, axis=2, keepdims=True)
    weight = jnp.where(visible, jnp.exp(score - highest), 0.0)
    total = jnp.sum(weight, axis=2)
    summed = jnp.einsum(
        "qtj,jd->tqd", weight.astype(bf16), values_all, preferred_element_type=f32
    )
    attended = (summed / total.T[:, :, None]).astype(bf16).reshape(tok, heads * head_dim)

    attended_all = jnp.stack(gather_rotated(attended, ctx_count))

    def share_of(index):
        rows = [
            lax.dynamic_index_in_dim(
                attended_all, (c - (index * per_share + j)) % ctx_count, 0, keepdims=False
            )
            for j in range(per_share)
        ]
        return jnp.concatenate(rows)

    low = e % 2
    half = exp_count // 2
    away = jnp.concatenate([share_of(1 - low + 2 * i) for i in range(half)])
    near = jnp.concatenate([share_of(low + 2 * i) for i in range(half)])
    sent = jnp.dot(away, out_weight, preferred_element_type=f32).astype(bf16)
    came = lax.ppermute(sent, "exp", [(i, i ^ 1) for i in range(exp_count)])
    acc = jnp.dot(near, out_weight, preferred_element_type=f32) + came.astype(f32)
    rows = per_share * tok
    for level in range(1, levels):
        bit = (e >> level) % 2
        half = half // 2
        acc = acc.reshape(half, 2, rows, width)
        sent = lax.dynamic_index_in_dim(acc, 1 - bit, 1, keepdims=False).astype(bf16)
        came = lax.ppermute(sent, "exp", [(i, i ^ (1 << level)) for i in range(exp_count)])
        acc = lax.dynamic_index_in_dim(acc, bit, 1, keepdims=False) + came.astype(f32)
    stream = acc.reshape(per_share, tok, width) + jnp.stack(residual_blocks).astype(f32)
    stream = stream.astype(bf16)

    pickers = []
    for k in range(exp_count):
        for j in range(per_share):
            block = lax.dynamic_index_in_dim(
                routes_stacked, (c - (e * per_share + j)) % ctx_count, 0, keepdims=False
            )
            pickers.append(picker_of(jnp.any(block == (e ^ k), axis=1), capacity).astype(bf16))
    pickers = lax.optimization_barrier(pickers)
    turns = sorted(range(ctx_count), key=lambda k: min(k, ctx_count - k))
    chunks, moved = {}, {}
    for k in turns:
        if k == turns[-1] and ctx_count > 2:
            chunk = lax.optimization_barrier((stream, moved[turns[0]][exp_count // 2]))[0]
        else:
            chunk = stream
        if k:
            chunk = lax.ppermute(chunk, "ctx", rotation(ctx_count, k))
        pieces = []
        for m in range(exp_count):
            picked = [
                jnp.dot(pickers[m * per_share + j], chunk[j], preferred_element_type=f32)
                for j in range(per_share)
            ]
            piece = jnp.concatenate(picked).astype(bf16)
            if m:
                piece = lax.ppermute(piece, "exp", [(i, i ^ m) for i in range(exp_count)])
            pieces.append(piece)
        moved[k] = pieces
        chunks[k] = jnp.concatenate(pieces)

    gate_here, up_here, down_here = expert_gate[0], expert_up[0], expert_down[0]
    for k in turns[-1:]:
        chunks[k] = lax.optimization_barrier(chunks[k])
    gate_proj = up_proj = squares = logits = 0.0
    for k in turns:
        chunk = chunks[k]
        start = ((c - k) % ctx_count) * width
        gate_rows = lax.dynamic_slice_in_dim(gate_here, start, width, 0)
        up_rows = lax.dynamic_slice_in_dim(up_here, start, width, 0)
        router_rows = lax.dynamic_slice_in_dim(router, start, width, 0)
        gate_proj += jnp.dot(chunk, gate_rows, preferred_element_type=f32)
        up_proj += jnp.dot(chunk, up_rows, preferred_element_type=f32)
        squares += jnp.sum(jnp.square(chunk.astype(f32)), axis=1, keepdims=True)
        logits += jnp.dot(chunk.astype(f32), router_rows, precision=lax.Precision.HIGHEST)
        gate_proj, up_proj, squares, logits = lax.optimization_barrier(
            (gate_proj, up_proj, squares, logits)
        )
    scale = lax.rsqrt(squares / features + 1e-05)
    act = (jax.nn.silu(gate_proj * scale) * (up_proj * scale)).astype(bf16)
    logits = logits * scale

    def rows_of(array, block):
        slot = ((e ^ (block // per_share)) * per_share + block % per_share) * capacity
        return lax.dynamic_slice_in_dim(array, slot, capacity, 0)

    own_rows = jnp.stack([rows_of(chunks[k], c) for k in range(ctx_count)])
    stream_rows = jnp.concatenate(
        [
            lax.dynamic_index_in_dim(own_rows, (c - a) % ctx_count, 0, keepdims=False)
            for a in range(ctx_count)
        ],
        axis=1,
    )

    experts = jnp.arange(router.shape[1], dtype=jnp.int32)
    mine = (experts == e).astype(f32)[None, :]
    own_share = tok // exp_count

    def contribution(k, gives, gated=False):
        block = (c + k) % ctx_count
        block_routes = routes_all[-k % ctx_count]
        picker = picker_of(jnp.any(block_routes == e, axis=1), capacity).astype(f32)
        other = jnp.sum(jnp.where(block_routes == e, 0, block_routes), axis=1)
        other_slot = jnp.dot(picker, (other[:, None] == experts[None, :]).astype(f32))
        gate = jax.nn.sigmoid(
            jnp.sum(rows_of(logits, block) * (mine - other_slot), axis=1, keepdims=True)
        )
        if gives is None:
            return gate
        if not gated:
            gives *= gate
        if k == 0:
            gives += 0.5 * stream_rows.astype(f32)
        gives = gives.astype(bf16)
        spread = picker.T.astype(bf16).reshape(exp_count // 2, 2, own_share, capacity)

        def spread_rows(bit):
            pick = lax.dynamic_index_in_dim(spread, bit, 1, keepdims=False)
            return jnp.dot(
                pick.reshape(tok // 2, capacity), gives, preferred_element_type=f32
            )

        sent = spread_rows(1 - low).astype(bf16)
        came = lax.ppermute(sent, "exp", [(i, i ^ 1) for i in range(exp_count)])
        first = came
        acc = spread_rows(low) + came.astype(f32)
        half = exp_count // 2
        for level in range(1, levels):
            bit = (e >> level) % 2
            half = half // 2
            acc = acc.reshape(half, 2, own_share, features)
            sent = lax.dynamic_index_in_dim(acc, 1 - bit, 1, keepdims=False).astype(bf16)
            came = lax.ppermute(sent, "exp", [(i, i ^ (1 << level)) for i in range(exp_count)])
            acc = lax.dynamic_index_in_dim(acc, bit, 1, keepdims=False) + came.astype(f32)
        return acc.reshape(own_share, features), first

    direct = [k for k in (1,) if k < ctx_count]
    others = [k for k in reversed(turns) if k and k not in direct]
    added, output, after = 0.0, 0.0, ()
    together = direct + others[:1]
    rows = jnp.concatenate([rows_of(act, (c + k) % ctx_count) for k in together])
    plain = jnp.ones((capacity, 1), f32)
    factor = jnp.concatenate([plain if k in direct else contribution(k, None) for k in together])
    shared = factor * jnp.dot(rows, down_here, preferred_element_type=f32)
    shared = dict(zip(together, jnp.split(shared.astype(bf16), len(together))))
    for k in direct:
        added += lax.ppermute(shared[k], "ctx", rotation(ctx_count, k)).astype(f32)
    for k in others:
        if k in shared:
            part, after = contribution(k, shared[k], gated=True)
        else:
            rows = rows_of(lax.optimization_barrier((act, after))[0], (c + k) % ctx_count)
            gives = jnp.dot(rows, down_here, preferred_element_type=f32)
            part, after = contribution(k, gives)
        part = part.astype(bf16)
        output += lax.ppermute(part, "ctx", rotation(ctx_count, k)).astype(f32)
    rows = rows_of(lax.optimization_barrier((act, after))[0], c)
    gives = jnp.dot(rows, down_here, preferred_element_type=f32)
    gives = lax.optimization_barrier(gives)
    part, _ = contribution(0, gives + added)
    return (output + part).astype(bf16)


def solution(mesh):
    return jax.shard_map(
        local,
        mesh=mesh,
        in_specs=(
            P(("groups", "ctx"), "exp"),
            P(("groups", "ctx"), "exp"),
            P(("groups", "ctx"), "exp"),
            P("exp", "ctx"),
            P(("groups", "ctx"), "exp"),
            P(),
            P(("groups", "ctx"), None),
            P(("groups", "ctx")),
            P("exp", None, "ctx"),
            P("exp", None, "ctx"),
            P("exp", "ctx", None),
        ),
        out_specs=P(("groups", "ctx", "exp"), None),
        check_vma=False,
    )
```
